128 devices in a mesh: tracer: 2 (over core), gx: 8 (over z, x_lo), gy: 8 (over x_hi, y).
Axes of the slice: x: 4 (x_hi: 2, x_lo: 2; x = x_hi * 2 + x_lo), y: 4, z: 4, core: 2. Of those that a mesh axis runs over, the one named last changes fastest.
Arguments:
- tracers: float32 [8, 16, 1024, 1024], P('tracer', None, 'gx', 'gy'), may hold values from -6 to 6
- wind_east: float32 [16, 1024, 1024], P(None, 'gx', 'gy'), may hold values from -0.2 to 0.2
- wind_north: float32 [16, 1024, 1024], P(None, 'gx', 'gy'), may hold values from -0.2 to 0.2
- diffusivity: float32 [16, 1024, 1024], P(None, 'gx', 'gy'), may hold values from 0.02 to 0.08
- emission: float32 [1024, 1024], P('gx', 'gy'), may hold values from 0.1 to 3
- region_tag: int32 [1024, 1024], P('gx', 'gy'), may hold values from 0 to 7
- footprint: float32 [8192, 80], P(('gx', 'gy')), may hold values from -4 to 4
- corners: int32 [8192, 2], P(('gx', 'gy')), may hold values from 0 to 992, as said below
- owner_map: int32 [64], replicated, may hold values from 0 to 63, each once
Outputs:
- stepped: float32 [8, 16, 1024, 1024], P('tracer', None, 'gx', 'gy')
- observed: float32 [8, 8192], P('tracer', ('gx', 'gy'))
The draws below stay inside these ranges and needn't reach their ends.
Inputs may be any that keep to these rules, and one draw needn't show every extreme that they name: Each observation's footprint lies inside the grid: corners[:, 0] <= 992 and corners[:, 1] <= 992. owner_map is a permutation.
All inputs are finite; a program needn't handle non-finite values.
Results may differ from the reference program's by a relative error of at most 0.0049.
Values sent between devices are 32-bit elements; how exact they have to be, the bound alone decides.
No kernel may reach another device: no remote copies, remote signals or barrier semaphores. Data moves between devices by JAX's collectives and lax.ppermute only.
A program may use at most 192 MiB of HBM per device.

```python
import math
import jax
import jax.numpy as jnp
from jax import lax

TRACERS = 8
NZ = 16
FP = 32
OBS_DEV = 128
NX = 1024
NY = 1024
BLOCKS = 64
OBS = 8192
N_GX = 8
N_GY = 8


def draw_corners(key, part):
    keys = jax.random.split(jax.random.fold_in(key, 7), 5)
    span_x = NX - FP
    span_y = NY - FP
    wide_x = jax.random.randint(keys[0], (OBS,), 0, span_x + 1)
    wide_y = jax.random.randint(keys[1], (OBS,), 0, span_y + 1)
    centre_x = jax.random.randint(keys[2], (OBS,), span_x // 4, 3 * span_x // 4 + 1)
    centre_y = jax.random.randint(keys[3], (OBS,), span_y // 4, 3 * span_y // 4 + 1)
    picks = jax.random.randint(keys[4], (OBS,), 0, 2)
    east = jnp.where(picks == 1, centre_x, wide_x)
    north = jnp.where(picks == 1, centre_y, wide_y)
    east = east.at[0].set(span_x).at[1].set(0)
    north = north.at[0].set(span_y).at[1].set(0)
    return jnp.stack([east, north], axis=1).astype(jnp.int32)


def plant(values, rng, smallest, top_value):
    index_at = [jax.random.randint(jax.random.fold_in(rng, axis), (), 0, length) for axis, length in enumerate(values.shape)]
    widest = values.shape.index(max(values.shape))
    beside = index_at[:widest] + [(index_at[widest] + 1) % values.shape[widest]] + index_at[widest + 1:]
    return values.at[tuple(index_at)].set(smallest).at[tuple(beside)].set(top_value)


def block_scale(rng, extent, cuts, smallest, top_value):
    factor_of, own = 1.0, jax.random.fold_in(rng, 6)
    for axis_at, shards_of in cuts:
        draws = jnp.exp(jax.random.uniform(jax.random.fold_in(own, axis_at), (shards_of,), jnp.float32, smallest / len(cuts), top_value / len(cuts)))
        factor_of = factor_of * jnp.repeat(draws, extent[axis_at] // shards_of).reshape([-1 if axis == axis_at else 1 for axis in range(len(extent))])
    return factor_of


def normal_values(rng, dims, deviation, most, shards=(), kind=jnp.bfloat16):
    result = deviation * jax.random.normal(rng, dims, jnp.float32)
    if shards:
        result = result * block_scale(rng, dims, shards, -0.22, 0.18)
    return jnp.clip(result, -most, most).astype(kind)


def setup_inputs(seed: int = 0) -> dict:
    seeds = jax.random.split(jax.random.key(seed), 10)
    tracers = normal_values(seeds[0], (TRACERS, NZ, NX, NY), 1.0, 6.0, ((0, 2), (2, 8), (3, 8)), jnp.float32)
    wind_east = jnp.clip(jax.random.uniform(seeds[1], (NZ, NX, NY), jnp.float32, -0.2, 0.2) * block_scale(seeds[1], (NZ, NX, NY), ((1, 8), (2, 8)), -0.4, 0.0), -0.2, 0.2)
    wind_north = jnp.clip(jax.random.uniform(seeds[2], (NZ, NX, NY), jnp.float32, -0.2, 0.2) * block_scale(seeds[2], (NZ, NX, NY), ((1, 8), (2, 8)), -0.4, 0.0), -0.2, 0.2)
    diffusivity = jnp.clip(jnp.exp(math.log(0.08) - 1.3862944 * jax.random.uniform(seeds[3], (NZ, NX, NY), jnp.float32) ** block_scale(seeds[3], (NZ, NX, NY), ((1, 8), (2, 8)), -0.2, 0.2)), 0.02, 0.08)
    emission = jnp.clip(jnp.exp(math.log(3.0) - 3.4011974 * jax.random.uniform(seeds[4], (NX, NY), jnp.float32) ** block_scale(seeds[4], (NX, NY), ((0, 8), (1, 8)), -0.2, 0.2)), 0.1, 3.0)
    region_tag = plant(jax.random.randint(seeds[5], (NX, NY), 0, TRACERS), jax.random.fold_in(seeds[5], 1), 0, TRACERS - 1).astype(jnp.int32)
    footprint = normal_values(seeds[6], (OBS, 2 * FP + NZ), 1.0, 4.0, ((0, 64),), jnp.float32)
    corners = draw_corners(jax.random.fold_in(seeds[9], 71), 0)
    owner_map = jax.random.permutation(seeds[8], N_GX * N_GY).astype(jnp.int32)
    return dict(tracers=tracers, wind_east=wind_east, wind_north=wind_north, diffusivity=diffusivity, emission=emission, region_tag=region_tag, footprint=footprint, corners=corners, owner_map=owner_map)


def face_flux(left, right, wind, kleft, kright):
    return jnp.maximum(wind, 0.0) * left + jnp.minimum(wind, 0.0) * right - 0.5 * (kleft + kright) * (right - left)

def reference(tracers, wind_east, wind_north, diffusivity, emission, region_tag, footprint, corners, owner_map):
    padded = jnp.pad(tracers, ((0, 0), (0, 0), (1, 1), (1, 1)))
    pad_east = jnp.pad(wind_east, ((0, 0), (1, 1), (1, 1)))[None]
    pad_north = jnp.pad(wind_north, ((0, 0), (1, 1), (1, 1)))[None]
    pad_diff = jnp.pad(diffusivity, ((0, 0), (1, 1), (1, 1)))[None]
    flux_x = face_flux(padded[:, :, :-1, 1:-1], padded[:, :, 1:, 1:-1], pad_east[:, :, :-1, 1:-1], pad_diff[:, :, :-1, 1:-1], pad_diff[:, :, 1:, 1:-1])
    flux_y = face_flux(padded[:, :, 1:-1, :-1], padded[:, :, 1:-1, 1:], pad_north[:, :, 1:-1, :-1], pad_diff[:, :, 1:-1, :-1], pad_diff[:, :, 1:-1, 1:])
    stepped = tracers - (flux_x[:, :, 1:] - flux_x[:, :, :-1]) - (flux_y[:, :, :, 1:] - flux_y[:, :, :, :-1])
    tagged = (jnp.arange(TRACERS, dtype=jnp.int32)[:, None, None] == region_tag[None]).astype(jnp.float32)
    stepped = stepped.at[:, 0].add(emission[None] * tagged)
    rounded = stepped.astype(jnp.bfloat16)
    along_x = footprint[:, :FP].astype(jnp.bfloat16).astype(jnp.float32)
    along_y = footprint[:, FP:2 * FP].astype(jnp.bfloat16).astype(jnp.float32)
    kernel = footprint[:, 2 * FP:]

    def window_sum(item):
        corner, prof_x, prof_y, kern = item
        zero = jnp.zeros((), jnp.int32)
        start = (zero, zero, corner[0].astype(jnp.int32), corner[1].astype(jnp.int32))
        window = lax.dynamic_slice(rounded, start, (TRACERS, NZ, FP, FP)).astype(jnp.float32)
        return jnp.einsum('tzab,a,b,z->t', window, prof_x, prof_y, kern, precision=lax.Precision.HIGHEST)

    def block_sum(items):
        return jax.vmap(window_sum)(items)
    blocks = (corners.reshape(BLOCKS, OBS_DEV, 2), along_x.reshape(BLOCKS, OBS_DEV, FP), along_y.reshape(BLOCKS, OBS_DEV, FP), kernel.reshape(BLOCKS, OBS_DEV, NZ))
    modelled = lax.map(block_sum, blocks) * (1.0 / (FP * math.sqrt(NZ)))
    modelled = jnp.transpose(modelled, (2, 0, 1))
    observed = jnp.zeros((TRACERS, BLOCKS, OBS_DEV), jnp.float32).at[:, owner_map].set(modelled)
    return (stepped, observed.reshape(TRACERS, OBS))
```

```python
import functools
import math

import jax
import jax.numpy as jnp
from jax import lax
from jax.experimental import pallas as pl
from jax.experimental.pallas import tpu as pltpu
from jax.sharding import PartitionSpec as P

FP = 32
CAP = 24
LANES = 128
TILES = ("gx", "gy")


def edges_kernel(nz, c_ref, we_ref, wn_ref, k_ref, e_ref, w_ref, n_ref, s_ref):
    count, zb = c_ref.shape[0], c_ref.shape[1]
    cols_x, cols_y = c_ref.shape[2], c_ref.shape[3]
    step = pl.program_id(0)

    @pl.when(step == 0)
    def _():
        n_ref[...] = jnp.zeros_like(n_ref)
        s_ref[...] = jnp.zeros_like(s_ref)

    lane = lax.broadcasted_iota(jnp.int32, n_ref.shape, 1)
    north = n_ref[...]
    south = s_ref[...]
    for zi in range(zb):
        z = step * zb + zi
        for t in range(count):
            slot = t * nz + z
            cells = c_ref[t, zi]
            e_ref[pl.ds(slot, 1), :] = c_ref[t, zi, cols_x - 1 : cols_x, :]
            w_ref[pl.ds(slot, 1), :] = c_ref[t, zi, 0:1, :]
            north = jnp.where(lane == slot, pltpu.roll(cells, slot + 1, 1), north)
            south = jnp.where(lane == slot, pltpu.roll(cells, slot, 1), south)
        slot = count * nz + z
        cells = k_ref[zi]
        e_ref[pl.ds(slot, 1), :] = k_ref[zi, cols_x - 1 : cols_x, :]
        w_ref[pl.ds(slot, 1), :] = k_ref[zi, 0:1, :]
        north = jnp.where(lane == slot, pltpu.roll(cells, slot + 1, 1), north)
        south = jnp.where(lane == slot, pltpu.roll(cells, slot, 1), south)
        slot = (count + 1) * nz + z
        e_ref[pl.ds(slot, 1), :] = we_ref[zi, cols_x - 1 : cols_x, :]
        north = jnp.where(lane == slot, pltpu.roll(wn_ref[zi], slot + 1, 1), north)
    n_ref[...] = north
    s_ref[...] = south


def edges(tracers, wind_east, wind_north, diffusivity):
    count, nz, cols_x, cols_y = tracers.shape
    zb = 4
    level = pl.BlockSpec((zb, cols_x, cols_y), lambda i: (i, 0, 0))
    rows_e = (count + 2) * nz
    rows_w = (count + 1) * nz
    f32 = jnp.float32
    return pl.pallas_call(
        functools.partial(edges_kernel, nz),
        grid=(nz // zb,),
        in_specs=[
            pl.BlockSpec((count, zb, cols_x, cols_y), lambda i: (0, i, 0, 0)),
            level,
            level,
            level,
        ],
        out_specs=[
            pl.BlockSpec((rows_e, cols_y), lambda i: (0, 0)),
            pl.BlockSpec((rows_w, cols_y), lambda i: (0, 0)),
            pl.BlockSpec((cols_x, LANES), lambda i: (0, 0)),
            pl.BlockSpec((cols_x, LANES), lambda i: (0, 0)),
        ],
        out_shape=[
            jax.ShapeDtypeStruct((rows_e, cols_y), f32),
            jax.ShapeDtypeStruct((rows_w, cols_y), f32),
            jax.ShapeDtypeStruct((cols_x, LANES), f32),
            jax.ShapeDtypeStruct((cols_x, LANES), f32),
        ],
        name="edges",
    )(tracers, wind_east, wind_north, diffusivity)


def step_kernel(
    nz, first_ref, c_ref, we_ref, wn_ref, k_ref, em_ref, tag_ref,
    hw_ref, he_ref, hs_ref, hn_ref, out_ref, r_ref,
):
    count = c_ref.shape[0]
    cols_x, cols_y = c_ref.shape[2], c_ref.shape[3]
    z = pl.program_id(0)
    row = lax.broadcasted_iota(jnp.int32, (cols_x, cols_y), 0)
    lane = lax.broadcasted_iota(jnp.int32, (cols_x, cols_y), 1)
    row_lo, row_hi = row == 0, row == cols_x - 1
    lane_lo, lane_hi = lane == 0, lane == cols_y - 1

    def from_west(a, slot):
        return jnp.where(row_lo, hw_ref[pl.ds(slot, 1), :], pltpu.roll(a, 1, 0))

    def from_east(a, slot):
        return jnp.where(row_hi, he_ref[pl.ds(slot, 1), :], pltpu.roll(a, cols_x - 1, 0))

    def from_south(a, slot):
        edge = pltpu.roll(hs_ref[...], LANES - slot, 1)
        return jnp.where(lane_lo, edge, pltpu.roll(a, 1, 1))

    def from_north(a, slot):
        edge = pltpu.roll(hn_ref[...], LANES - 1 - slot, 1)
        return jnp.where(lane_hi, edge, pltpu.roll(a, cols_y - 1, 1))

    we, wn, k = we_ref[0], wn_ref[0], k_ref[0]
    at_k, at_w = count * nz + z, (count + 1) * nz + z
    d_e = 0.5 * (k + from_east(k, at_k))
    d_n = 0.5 * (k + from_north(k, at_k))
    d_w = 0.5 * (k + from_west(k, at_k))
    d_s = 0.5 * (k + from_south(k, at_k))
    we_m = from_west(we, at_w)
    wn_m = from_south(wn, at_w)
    a_e, b_e = jnp.maximum(we, 0.0) + d_e, jnp.minimum(we, 0.0) - d_e
    a_n, b_n = jnp.maximum(wn, 0.0) + d_n, jnp.minimum(wn, 0.0) - d_n
    a_w, b_w = jnp.maximum(we_m, 0.0) + d_w, jnp.minimum(we_m, 0.0) - d_w
    a_s, b_s = jnp.maximum(wn_m, 0.0) + d_s, jnp.minimum(wn_m, 0.0) - d_s
    middle = 1.0 - (a_e - b_w) - (a_n - b_s)
    for t in range(count):
        c = c_ref[t, 0]
        slot = t * nz + z
        new = (
            middle * c
            - b_e * from_east(c, slot)
            + a_w * from_west(c, slot)
            - b_n * from_north(c, slot)
            + a_s * from_south(c, slot)
        )
        out_ref[t, 0] = new

    @pl.when(z == 0)
    def _():
        for t in range(count):
            hit = tag_ref[...] == first_ref[0] + t
            out_ref[t, 0] = out_ref[t, 0] + jnp.where(hit, em_ref[...], 0.0)

    for t in range(count):
        r_ref[:, t * cols_y : (t + 1) * cols_y] = out_ref[t, 0].astype(jnp.bfloat16)


def advance(first, tracers, wind_east, wind_north, diffusivity, emission, tag, halos):
    count, nz, cols_x, cols_y = tracers.shape
    level = pl.BlockSpec((1, cols_x, cols_y), lambda z: (z, 0, 0))

    def whole(a):
        return pl.BlockSpec(a.shape, lambda z: (0, 0))

    fields = pl.BlockSpec((count, 1, cols_x, cols_y), lambda z: (0, z, 0, 0))
    return pl.pallas_call(
        functools.partial(step_kernel, nz),
        grid=(nz,),
        in_specs=[
            pl.BlockSpec(memory_space=pltpu.SMEM),
            fields,
            level,
            level,
            level,
            whole(emission),
            whole(tag),
            *[whole(h) for h in halos],
        ],
        out_specs=[fields, pl.BlockSpec((cols_x, count * cols_y), lambda z: (z, 0))],
        out_shape=[
            jax.ShapeDtypeStruct(tracers.shape, jnp.float32),
            jax.ShapeDtypeStruct((nz * cols_x, count * cols_y), jnp.bfloat16),
        ],
        cost_estimate=pl.CostEstimate(
            flops=40 * tracers.size, bytes_accessed=13 << 20, transcendentals=0
        ),
        name="advance",
    )(first, tracers, wind_east, wind_north, diffusivity, emission, tag, *halos)


def pack_kernel(tiles_x, tiles_y, size, nz, round_ref, fp_ref, corner_ref, corner_t_ref, out_ref, m_ref):
    tiles = tiles_x * tiles_y
    obs = fp_ref.shape[0]
    tile = lax.broadcasted_iota(jnp.int32, (tiles, obs), 0)
    first_x = (tile // tiles_y) * size[0]
    first_y = (tile % tiles_y) * size[1]
    x0 = corner_t_ref[0:1, :]
    y0 = corner_t_ref[1:2, :]
    touch = (
        (x0 < first_x + size[0])
        & (x0 + FP > first_x)
        & (y0 < first_y + size[1])
        & (y0 + FP > first_y)
    )
    ones = jnp.where(touch, 1.0, 0.0)
    before = lax.broadcasted_iota(jnp.int32, (obs, obs), 0) < lax.broadcasted_iota(
        jnp.int32, (obs, obs), 1
    )
    rank = jnp.dot(
        ones.astype(jnp.bfloat16),
        jnp.where(before, 1.0, 0.0).astype(jnp.bfloat16),
        preferred_element_type=jnp.float32,
    ).astype(jnp.int32)
    most = jnp.max(jnp.sum(ones, axis=1, keepdims=True), axis=0, keepdims=True)
    slot = jnp.where(touch, rank - round_ref[0] * CAP, -1)
    which = lax.broadcasted_iota(jnp.int32, (tiles, CAP, obs), 1)
    pick = jnp.where(slot[:, None, :] == which, 1.0, 0.0).reshape(tiles * CAP, obs)
    pick = pick.astype(jnp.bfloat16)

    width = 2 * FP + nz
    lane = lax.broadcasted_iota(jnp.int32, (obs, LANES), 1)
    m_ref[...] = jnp.zeros_like(m_ref)
    m_ref[:, 0:width] = fp_ref[...]
    corner = corner_ref[...].astype(jnp.float32)
    rows = m_ref[...]
    rows = jnp.where(lane == width, corner[:, 0:1], rows)
    rows = jnp.where(lane == width + 1, corner[:, 1:2], rows)
    rows = jnp.where(
        lane == width + 2,
        lax.broadcasted_iota(jnp.int32, (obs, LANES), 0).astype(jnp.float32),
        rows,
    )
    high = rows.astype(jnp.bfloat16)
    low = jnp.where(lane < 2 * FP, 0.0, rows - high.astype(jnp.float32)).astype(jnp.bfloat16)
    packed = jnp.dot(pick, high, preferred_element_type=jnp.float32) + jnp.dot(
        pick, low, preferred_element_type=jnp.float32
    )
    lane_all = lax.broadcasted_iota(jnp.int32, packed.shape, 1)
    packed = jnp.where(lane_all == width + 3, most, packed)
    out_ref[...] = packed


def pack(number, footprint, corners, tiles_x, tiles_y, size):
    obs, width = footprint.shape
    nz = width - 2 * FP
    tiles = tiles_x * tiles_y
    vmem = pl.BlockSpec(memory_space=pltpu.VMEM)
    return pl.pallas_call(
        functools.partial(pack_kernel, tiles_x, tiles_y, size, nz),
        in_specs=[pl.BlockSpec(memory_space=pltpu.SMEM), vmem, vmem, vmem],
        out_specs=vmem,
        out_shape=jax.ShapeDtypeStruct((tiles * CAP, LANES), jnp.float32),
        scratch_shapes=[pltpu.VMEM((obs, LANES), jnp.float32)],
        compiler_params=pltpu.CompilerParams(vmem_limit_bytes=32 << 20),
        name="pack",
    )(number, footprint, corners, corners.T)


def observe_kernel(nz, sources, origin_ref, owner_ref, rows_ref, r_ref, out_ref, most_ref, w_ref):
    count = out_ref.shape[1]
    cols = LANES
    group = 16
    chunk = group * CAP
    scale = 1.0 / (FP * math.sqrt(nz))
    width = 2 * FP + nz

    def body(step, most):
        rows = rows_ref[pl.ds(pl.multiple_of(step * chunk, chunk), chunk), :]
        lane = lax.broadcasted_iota(jnp.int32, (chunk, cols), 1)

        def along(at, place, origin):
            offset = lane - (rows[:, place : place + 1].astype(jnp.int32) - origin)
            inside = (offset >= 0) & (offset < FP)
            taken = jnp.take_along_axis(rows, jnp.clip(offset, 0, FP - 1) + at, axis=1)
            return jnp.where(inside, taken, 0.0)

        wx = along(0, width, origin_ref[0])
        wy = along(FP, width + 1, origin_ref[1]) * scale
        for z in range(nz):
            part = wx * rows[:, 2 * FP + z : 2 * FP + z + 1]
            w_ref[:, z * cols : (z + 1) * cols] = part.astype(jnp.bfloat16)
        got = jnp.dot(w_ref[...], r_ref[...], preferred_element_type=jnp.float32)
        mine = rows[:, width + 2 : width + 3].astype(jnp.int32) == lane
        for t in range(count):
            value = jnp.sum(got[:, t * cols : (t + 1) * cols] * wy, axis=1, keepdims=True)
            spread = jnp.where(mine, value, 0.0).reshape(group, CAP, cols)
            spread = jnp.sum(spread, axis=1)
            for g in range(group):
                out_ref[owner_ref[step * group + g], t : t + 1, :] = spread[g : g + 1, :]
        return jnp.maximum(most, jnp.max(rows[:, width + 3 : width + 4], axis=0, keepdims=True))

    most = lax.fori_loop(0, sources // group, body, jnp.zeros((1, 1), jnp.float32))
    most_ref[...] = jnp.broadcast_to(most, most_ref.shape).astype(jnp.int32)


def observe(origin, owner_map, rows, rounded, count, nz):
    sources = owner_map.shape[0]
    vmem = pl.BlockSpec(memory_space=pltpu.VMEM)
    smem = pl.BlockSpec(memory_space=pltpu.SMEM)
    return pl.pallas_call(
        functools.partial(observe_kernel, nz, sources),
        in_specs=[smem, smem, vmem, vmem],
        out_specs=[vmem, vmem],
        out_shape=[
            jax.ShapeDtypeStruct((sources, count, LANES), jnp.float32),
            jax.ShapeDtypeStruct((8, LANES), jnp.int32),
        ],
        scratch_shapes=[pltpu.VMEM((16 * CAP, rounded.shape[0]), jnp.bfloat16)],
        compiler_params=pltpu.CompilerParams(vmem_limit_bytes=48 << 20),
        name="observe",
    )(origin, owner_map, rows, rounded)


def per_device(
    tracers, wind_east, wind_north, diffusivity, emission, region_tag, footprint, corners, owner_map
):
    count, nz, cols_x, cols_y = tracers.shape
    tiles_x, tiles_y = lax.axis_size("gx"), lax.axis_size("gy")
    tiles = tiles_x * tiles_y
    obs = footprint.shape[0]

    east, west, north, south = edges(tracers, wind_east, wind_north, diffusivity)
    up_x = [(i, i + 1) for i in range(tiles_x - 1)]
    up_y = [(i, i + 1) for i in range(tiles_y - 1)]
    halos = (
        lax.ppermute(east, "gx", up_x),
        lax.ppermute(west, "gx", [(b, a) for a, b in up_x]),
        lax.ppermute(north, "gy", up_y),
        lax.ppermute(south, "gy", [(b, a) for a, b in up_y]),
    )
    first = (lax.axis_index("tracer") * count).astype(jnp.int32).reshape(1)
    stepped, rounded = advance(
        first, tracers, wind_east, wind_north, diffusivity, emission, region_tag, halos
    )
    origin = jnp.stack([lax.axis_index("gx") * cols_x, lax.axis_index("gy") * cols_y])
    origin = origin.astype(jnp.int32)

    def one_round(number):
        sent = pack(
            jnp.reshape(number, (1,)).astype(jnp.int32),
            footprint, corners, tiles_x, tiles_y, (cols_x, cols_y),
        )
        rows = lax.all_to_all(sent.reshape(tiles, CAP, LANES), TILES, 0, 0)
        parts, most = observe(
            origin, owner_map, rows.reshape(tiles * CAP, LANES), rounded, count, nz
        )
        parts = lax.all_to_all(parts, TILES, 0, 0)
        return jnp.sum(parts, axis=0), most[0, 0]

    observed, most = one_round(jnp.int32(0))
    rounds = (most + CAP - 1) // CAP
    observed = lax.fori_loop(
        jnp.int32(1), rounds, lambda r, total: total + one_round(r)[0], observed
    )
    return (stepped, observed)


def solution(mesh):
    return jax.shard_map(
        per_device,
        mesh=mesh,
        in_specs=(
            P("tracer", None, "gx", "gy"),
            P(None, "gx", "gy"),
            P(None, "gx", "gy"),
            P(None, "gx", "gy"),
            P("gx", "gy"),
            P("gx", "gy"),
            P(("gx", "gy"), None),
            P(("gx", "gy"), None),
            P(),
        ),
        out_specs=(P("tracer", None, "gx", "gy"), P("tracer", ("gx", "gy"))),
        check_vma=False,
    )
```

```python
import functools
import math

import jax
import jax.numpy as jnp
from jax import lax
from jax.experimental import pallas as pl
from jax.experimental.pallas import tpu as pltpu
from jax.sharding import PartitionSpec as P

FP = 32
CAP = 24
LANES = 128
TILES = ("gx", "gy")


def edges_kernel(
    nz, c_ref, we_ref, wn_ref, k_ref, e_ref, w_ref, n_ref, s_ref, ct_ref, wnt_ref, kt_ref
):
    count, zb = c_ref.shape[0], c_ref.shape[1]
    cols_x, cols_y = c_ref.shape[2], c_ref.shape[3]
    step = pl.program_id(0)

    def ends(slot, cells, flipped):
        e_ref[pl.ds(slot, 1), :] = cells[cols_x - 1 : cols_x, :]
        w_ref[pl.ds(slot, 1), :] = cells[0:1, :]
        n_ref[pl.ds(slot, 1), :] = flipped[cols_y - 1 : cols_y, :]
        s_ref[pl.ds(slot, 1), :] = flipped[0:1, :]

    for zi in range(zb):
        z = step * zb + zi
        for t in range(count):
            cells = c_ref[t, zi]
            flipped = cells.T
            ct_ref[t, zi] = flipped
            ends(t * nz + z, cells, flipped)
        cells = k_ref[zi]
        flipped = cells.T
        kt_ref[zi] = flipped
        ends(count * nz + z, cells, flipped)
        slot = (count + 1) * nz + z
        flipped = wn_ref[zi].T
        wnt_ref[zi] = flipped
        e_ref[pl.ds(slot, 1), :] = we_ref[zi, cols_x - 1 : cols_x, :]
        n_ref[pl.ds(slot, 1), :] = flipped[cols_y - 1 : cols_y, :]


def edges(tracers, wind_east, wind_north, diffusivity):
    count, nz, cols_x, cols_y = tracers.shape
    zb = 4
    f32 = jnp.float32
    level = pl.BlockSpec((zb, cols_x, cols_y), lambda i: (i, 0, 0))
    fields = pl.BlockSpec((count, zb, cols_x, cols_y), lambda i: (0, i, 0, 0))
    flat = [(count + 2, cols_y), (count + 1, cols_y), (count + 2, cols_x), (count + 1, cols_x)]
    return pl.pallas_call(
        functools.partial(edges_kernel, nz),
        grid=(nz // zb,),
        in_specs=[fields, level, level, level],
        out_specs=[
            *[pl.BlockSpec((n * nz, width), lambda i: (0, 0)) for n, width in flat],
            pl.BlockSpec((count, zb, cols_y, cols_x), lambda i: (0, i, 0, 0)),
            pl.BlockSpec((zb, cols_y, cols_x), lambda i: (i, 0, 0)),
            pl.BlockSpec((zb, cols_y, cols_x), lambda i: (i, 0, 0)),
        ],
        out_shape=[
            *[jax.ShapeDtypeStruct((n * nz, width), f32) for n, width in flat],
            jax.ShapeDtypeStruct((count, nz, cols_y, cols_x), f32),
            jax.ShapeDtypeStruct((nz, cols_y, cols_x), f32),
            jax.ShapeDtypeStruct((nz, cols_y, cols_x), f32),
        ],
        compiler_params=pltpu.CompilerParams(vmem_limit_bytes=24 << 20),
        name="edges",
    )(tracers, wind_east, wind_north, diffusivity)


def step_kernel(
    nz, first_ref, c_ref, ct_ref, we_ref, wnt_ref, k_ref, kt_ref, em_ref, tag_ref,
    hw_ref, he_ref, hs_ref, hn_ref, out_ref, r_ref,
):
    count, zb = c_ref.shape[0], c_ref.shape[1]
    cols_x, cols_y = c_ref.shape[2], c_ref.shape[3]
    step = pl.program_id(0)

    def before(a, halo_ref, slot):
        row = lax.broadcasted_iota(jnp.int32, a.shape, 0)
        return jnp.where(row == 0, halo_ref[pl.ds(slot, 1), :], pltpu.roll(a, 1, 0))

    def after(a, halo_ref, slot):
        last = a.shape[0] - 1
        row = lax.broadcasted_iota(jnp.int32, a.shape, 0)
        return jnp.where(row == last, halo_ref[pl.ds(slot, 1), :], pltpu.roll(a, last, 0))

    def coefficients(wind, k, low_ref, high_ref, z):
        at_k, at_w = count * nz + z, (count + 1) * nz + z
        mix = 0.5 * (k + after(k, high_ref, at_k))
        mix_m = 0.5 * (k + before(k, low_ref, at_k))
        wind_m = before(wind, low_ref, at_w)
        own = jnp.maximum(wind, 0.0) + mix - (jnp.minimum(wind_m, 0.0) - mix_m)
        return own, mix - jnp.minimum(wind, 0.0), jnp.maximum(wind_m, 0.0) + mix_m

    for zi in range(zb):
        z = step * zb + zi
        own_x, next_x, prev_x = coefficients(we_ref[zi], k_ref[zi], hw_ref, he_ref, z)
        own_y, next_y, prev_y = coefficients(wnt_ref[zi], kt_ref[zi], hs_ref, hn_ref, z)
        own_x = 1.0 - own_x
        for t in range(count):
            slot = t * nz + z
            ct = ct_ref[t, zi]
            part_y = (
                next_y * after(ct, hn_ref, slot) + prev_y * before(ct, hs_ref, slot) - own_y * ct
            )
            c = c_ref[t, zi]
            part_x = (
                own_x * c + next_x * after(c, he_ref, slot) + prev_x * before(c, hw_ref, slot)
            )
            new = part_x + part_y.T
            if zi == 0:
                hit = (tag_ref[...] == first_ref[0] + t) & (step == 0)
                new = new + jnp.where(hit, em_ref[...], 0.0)
            out_ref[t, zi] = new
            r_ref[t * cols_y : (t + 1) * cols_y, zi * cols_x : (zi + 1) * cols_x] = new.T.astype(
                jnp.bfloat16
            )


def advance(first, tracers, tracers_t, wind_east, wind_north_t, k, k_t, emission, tag, halos):
    count, nz, cols_x, cols_y = tracers.shape
    zb = 2
    level = pl.BlockSpec((zb, cols_x, cols_y), lambda i: (i, 0, 0))
    level_t = pl.BlockSpec((zb, cols_y, cols_x), lambda i: (i, 0, 0))

    def whole(a):
        return pl.BlockSpec(a.shape, lambda i: (0, 0))

    fields = pl.BlockSpec((count, zb, cols_x, cols_y), lambda i: (0, i, 0, 0))
    fields_t = pl.BlockSpec((count, zb, cols_y, cols_x), lambda i: (0, i, 0, 0))
    return pl.pallas_call(
        functools.partial(step_kernel, nz),
        grid=(nz // zb,),
        in_specs=[
            pl.BlockSpec(memory_space=pltpu.SMEM),
            fields,
            fields_t,
            level,
            level_t,
            level,
            level_t,
            whole(emission),
            whole(tag),
            *[whole(h) for h in halos],
        ],
        out_specs=[fields, pl.BlockSpec((count * cols_y, zb * cols_x), lambda i: (0, i))],
        out_shape=[
            jax.ShapeDtypeStruct(tracers.shape, jnp.float32),
            jax.ShapeDtypeStruct((count * cols_y, nz * cols_x), jnp.bfloat16),
        ],
        cost_estimate=pl.CostEstimate(
            flops=40 * tracers.size, bytes_accessed=18 << 20, transcendentals=0
        ),
        compiler_params=pltpu.CompilerParams(vmem_limit_bytes=24 << 20),
        name="advance",
    )(first, tracers, tracers_t, wind_east, wind_north_t, k, k_t, emission, tag, *halos)


def pack_kernel(
    tiles_x, tiles_y, size, nz, number_ref, owner_ref, fp_ref, corner_ref, out_ref, m_ref
):
    tiles = tiles_x * tiles_y
    obs = fp_ref.shape[1]
    width = 2 * FP + nz
    tile = lax.broadcasted_iota(jnp.int32, (tiles, obs), 0)
    first_x = (tile // tiles_y) * size[0]
    first_y = (tile % tiles_y) * size[1]
    x0 = corner_ref[0:1, :]
    y0 = corner_ref[1:2, :]
    touch = (
        (x0 < first_x + size[0])
        & (x0 + FP > first_x)
        & (y0 < first_y + size[1])
        & (y0 + FP > first_y)
    )
    ones = jnp.where(touch, 1.0, 0.0)
    earlier = lax.broadcasted_iota(jnp.int32, (obs, obs), 0) < lax.broadcasted_iota(
        jnp.int32, (obs, obs), 1
    )
    rank = jnp.dot(
        ones.astype(jnp.bfloat16),
        jnp.where(earlier, 1.0, 0.0).astype(jnp.bfloat16),
        preferred_element_type=jnp.float32,
    ).astype(jnp.int32)
    most = jnp.max(jnp.sum(ones, axis=1, keepdims=True), axis=0, keepdims=True)
    slot = jnp.where(touch, rank - number_ref[0] * CAP, -1)
    which = lax.broadcasted_iota(jnp.int32, (tiles, CAP, obs), 1)
    pick = jnp.where(slot[:, None, :] == which, 1.0, 0.0).reshape(tiles * CAP, obs)
    pick = pick.astype(jnp.bfloat16)

    def rotated(profile, by):
        shift = 1
        while shift < FP:
            turn = (by & shift) != 0
            profile = jnp.where(turn, pltpu.roll(profile, shift, 0), profile)
            shift *= 2
        return profile

    m_ref[0:FP, :] = rotated(fp_ref[0:FP, :], x0)
    m_ref[FP : 2 * FP, :] = rotated(fp_ref[FP : 2 * FP, :], y0)
    m_ref[2 * FP : width, :] = fp_ref[2 * FP : width, :]
    m_ref[width:, :] = jnp.zeros_like(m_ref[width:, :])
    m_ref[width : width + 2, :] = corner_ref[...].astype(jnp.float32)
    m_ref[width + 2 : width + 3, :] = lax.broadcasted_iota(jnp.int32, (1, obs), 1).astype(
        jnp.float32
    )
    rows = m_ref[...].T
    lane = lax.broadcasted_iota(jnp.int32, rows.shape, 1)
    high = rows.astype(jnp.bfloat16)
    low = jnp.where(lane < 2 * FP, 0.0, rows - high.astype(jnp.float32)).astype(jnp.bfloat16)
    packed = jnp.dot(pick, high, preferred_element_type=jnp.float32) + jnp.dot(
        pick, low, preferred_element_type=jnp.float32
    )
    lane = lax.broadcasted_iota(jnp.int32, packed.shape, 1)
    packed = jnp.where(lane == width + 3, most, packed)
    owner = owner_ref[number_ref[1]].astype(jnp.float32)
    out_ref[...] = jnp.where(lane == width + 4, owner, packed)


def pack(number, owner_map, footprint, corners, tiles_x, tiles_y, size):
    obs, width = footprint.shape
    nz = width - 2 * FP
    tiles = tiles_x * tiles_y
    vmem = pl.BlockSpec(memory_space=pltpu.VMEM)
    smem = pl.BlockSpec(memory_space=pltpu.SMEM)
    return pl.pallas_call(
        functools.partial(pack_kernel, tiles_x, tiles_y, size, nz),
        in_specs=[smem, smem, vmem, vmem],
        out_specs=vmem,
        out_shape=jax.ShapeDtypeStruct((tiles * CAP, LANES), jnp.float32),
        scratch_shapes=[pltpu.VMEM((LANES, obs), jnp.float32)],
        compiler_params=pltpu.CompilerParams(vmem_limit_bytes=24 << 20),
        name="pack",
    )(number, owner_map, footprint.T, corners.T)


def observe_kernel(nz, count, origin_ref, rows_ref, r_ref, out_ref, most_ref, w_ref):
    cols = LANES
    chunk = w_ref.shape[1]
    scale = 1.0 / (FP * math.sqrt(nz))
    width = 2 * FP + nz
    out_ref[...] = jnp.zeros_like(out_ref)

    def body(step, most):
        rows = rows_ref[pl.ds(pl.multiple_of(step * chunk, chunk), chunk), :].T
        place = lax.broadcasted_iota(jnp.int32, (cols, chunk), 0)

        def along(profile, corner, origin):
            offset = place - (corner.astype(jnp.int32) - origin)
            inside = (offset >= 0) & (offset < FP)
            return jnp.where(inside, jnp.concatenate([profile] * (cols // FP), axis=0), 0.0)

        wx = along(rows[0:FP], rows[width : width + 1], origin_ref[0])
        for z in range(nz):
            part = wx * rows[2 * FP + z : 2 * FP + z + 1]
            w_ref[z * cols : (z + 1) * cols, :] = part.astype(jnp.bfloat16)
        got = jnp.dot(r_ref[...], w_ref[...], preferred_element_type=jnp.float32)
        wy = along(rows[FP : 2 * FP], rows[width + 1 : width + 2], origin_ref[1]) * scale
        values = [
            jnp.sum(got[t * cols : (t + 1) * cols] * wy, axis=0, keepdims=True)
            for t in range(count)
        ]
        values = jnp.concatenate(values * (8 // count), axis=0)
        lines = out_ref.shape[0]
        owner = lax.broadcasted_iota(jnp.int32, (lines, chunk), 0) // count
        mine = owner == rows[width + 4 : width + 5].astype(jnp.int32)
        spread = jnp.where(mine, jnp.concatenate([values] * (lines // 8), axis=0), 0.0)
        high = spread.astype(jnp.bfloat16)
        low = (spread - high.astype(jnp.float32)).astype(jnp.bfloat16)
        obs = jnp.where(place == rows[width + 2 : width + 3].astype(jnp.int32), 1.0, 0.0)
        obs = obs.astype(jnp.bfloat16)
        across = (((1,), (1,)), ((), ()))
        out_ref[...] += lax.dot_general(
            high, obs, across, preferred_element_type=jnp.float32
        ) + lax.dot_general(low, obs, across, preferred_element_type=jnp.float32)
        return jnp.maximum(most, jnp.max(rows[width + 3 : width + 4], axis=1, keepdims=True))

    chunks = rows_ref.shape[0] // chunk
    most = lax.fori_loop(0, chunks, body, jnp.zeros((1, 1), jnp.float32))
    most_ref[...] = jnp.broadcast_to(most, most_ref.shape).astype(jnp.int32)


def observe(origin, rows, rounded, count, nz, sources):
    vmem = pl.BlockSpec(memory_space=pltpu.VMEM)
    smem = pl.BlockSpec(memory_space=pltpu.SMEM)
    return pl.pallas_call(
        functools.partial(observe_kernel, nz, count),
        in_specs=[smem, vmem, vmem],
        out_specs=[vmem, vmem],
        out_shape=[
            jax.ShapeDtypeStruct((sources * count, LANES), jnp.float32),
            jax.ShapeDtypeStruct((8, LANES), jnp.int32),
        ],
        scratch_shapes=[pltpu.VMEM((rounded.shape[1], 512), jnp.bfloat16)],
        compiler_params=pltpu.CompilerParams(vmem_limit_bytes=24 << 20),
        name="observe",
    )(origin, rows, rounded)


def per_device(
    tracers, wind_east, wind_north, diffusivity, emission, region_tag, footprint, corners, owner_map
):
    count, nz, cols_x, cols_y = tracers.shape
    tiles_x, tiles_y = lax.axis_size("gx"), lax.axis_size("gy")
    tiles = tiles_x * tiles_y
    obs = footprint.shape[0]

    east, west, north, south, tracers_t, wind_north_t, k_t = edges(
        tracers, wind_east, wind_north, diffusivity
    )
    up_x = [(i, i + 1) for i in range(tiles_x - 1)]
    up_y = [(i, i + 1) for i in range(tiles_y - 1)]
    halos = (
        lax.ppermute(east, "gx", up_x),
        lax.ppermute(west, "gx", [(b, a) for a, b in up_x]),
        lax.ppermute(north, "gy", up_y),
        lax.ppermute(south, "gy", [(b, a) for a, b in up_y]),
    )
    first = (lax.axis_index("tracer") * count).astype(jnp.int32).reshape(1)
    stepped, rounded = advance(
        first, tracers, tracers_t, wind_east, wind_north_t, diffusivity, k_t,
        emission, region_tag, halos,
    )
    origin = jnp.stack([lax.axis_index("gx") * cols_x, lax.axis_index("gy") * cols_y])
    origin = origin.astype(jnp.int32)
    me = lax.axis_index(TILES).astype(jnp.int32)

    def one_round(number):
        sent = pack(
            jnp.stack([number, me]), owner_map, footprint, corners, tiles_x, tiles_y, (cols_x, cols_y),
        )
        rows = lax.all_to_all(sent.reshape(tiles, CAP, LANES), TILES, 0, 0)
        parts, most = observe(
            origin, rows.reshape(tiles * CAP, LANES), rounded, count, nz, tiles
        )
        parts = lax.all_to_all(parts.reshape(tiles, count, obs), TILES, 0, 0)
        return jnp.sum(parts, axis=0), most[0, 0]

    observed, most = one_round(jnp.int32(0))
    rounds = (most + CAP - 1) // CAP
    observed = lax.fori_loop(
        jnp.int32(1), rounds, lambda r, total: total + one_round(r)[0], observed
    )
    return (stepped, observed)


def solution(mesh):
    return jax.shard_map(
        per_device,
        mesh=mesh,
        in_specs=(
            P("tracer", None, "gx", "gy"),
            P(None, "gx", "gy"),
            P(None, "gx", "gy"),
            P(None, "gx", "gy"),
            P("gx", "gy"),
            P("gx", "gy"),
            P(("gx", "gy"), None),
            P(("gx", "gy"), None),
            P(),
        ),
        out_specs=(P("tracer", None, "gx", "gy"), P("tracer", ("gx", "gy"))),
        check_vma=False,
    )
```

```python
import functools
import math

import jax
import jax.numpy as jnp
from jax import lax
from jax.experimental import pallas as pl
from jax.experimental.pallas import tpu as pltpu
from jax.sharding import PartitionSpec as P

FP = 32
CAP = 24
LANES = 128
CHUNK = 256
VMEM_ALL = 56 << 20
VMEM_MOST = 52 << 20
TILES = ("gx", "gy")


def pack_kernel(
    tiles_x, tiles_y, size, nz, number_ref, owner_ref, fp_ref, corner_ref, out_ref, m_ref
):
    tiles = tiles_x * tiles_y
    obs = fp_ref.shape[1]
    width = 2 * FP + nz
    tile = lax.broadcasted_iota(jnp.int32, (tiles, obs), 0)
    first_x = (tile // tiles_y) * size[0]
    first_y = (tile % tiles_y) * size[1]
    x0 = corner_ref[0:1, :]
    y0 = corner_ref[1:2, :]
    touch = (
        (x0 < first_x + size[0])
        & (x0 + FP > first_x)
        & (y0 < first_y + size[1])
        & (y0 + FP > first_y)
    )
    ones = jnp.where(touch, 1.0, 0.0)
    earlier = lax.broadcasted_iota(jnp.int32, (obs, obs), 0) < lax.broadcasted_iota(
        jnp.int32, (obs, obs), 1
    )
    rank = jnp.dot(
        ones.astype(jnp.bfloat16),
        jnp.where(earlier, 1.0, 0.0).astype(jnp.bfloat16),
        preferred_element_type=jnp.float32,
    ).astype(jnp.int32)
    count = jnp.sum(ones, axis=1, keepdims=True)
    most = jnp.max(count, axis=0, keepdims=True)
    now = jnp.clip(count - (number_ref[0] * CAP).astype(jnp.float32), 0.0, CAP)
    slot = jnp.where(touch, rank - number_ref[0] * CAP, -1)
    which = lax.broadcasted_iota(jnp.int32, (tiles, CAP, obs), 1)
    pick = jnp.where(slot[:, None, :] == which, 1.0, 0.0).reshape(tiles * CAP, obs)
    pick = pick.astype(jnp.bfloat16)

    def rotated(profile, by):
        shift = 1
        while shift < FP:
            turn = (by & shift) != 0
            profile = jnp.where(turn, pltpu.roll(profile, shift, 0), profile)
            shift *= 2
        return profile

    m_ref[0:FP, :] = rotated(fp_ref[0:FP, :], x0)
    m_ref[FP : 2 * FP, :] = rotated(fp_ref[FP : 2 * FP, :], y0)
    m_ref[2 * FP : width, :] = fp_ref[2 * FP : width, :]
    m_ref[width:, :] = jnp.zeros_like(m_ref[width:, :])
    m_ref[width : width + 2, :] = corner_ref[...].astype(jnp.float32)
    m_ref[width + 2 : width + 3, :] = lax.broadcasted_iota(jnp.int32, (1, obs), 1).astype(
        jnp.float32
    )
    rows = m_ref[...].T
    lane = lax.broadcasted_iota(jnp.int32, rows.shape, 1)
    high = rows.astype(jnp.bfloat16)
    low = jnp.where(lane < 2 * FP, 0.0, rows - high.astype(jnp.float32)).astype(jnp.bfloat16)
    packed = jnp.dot(pick, high, preferred_element_type=jnp.float32) + jnp.dot(
        pick, low, preferred_element_type=jnp.float32
    )
    lane = lax.broadcasted_iota(jnp.int32, packed.shape, 1)
    packed = jnp.where(lane == width + 3, most, packed)
    owner = owner_ref[number_ref[1]].astype(jnp.float32)
    packed = jnp.where(lane == width + 4, owner, packed)
    now = jnp.broadcast_to(now[:, :, None], (tiles, CAP, LANES)).reshape(packed.shape)
    out_ref[...] = jnp.where(lane == width + 5, now, packed)


def pack(number, owner_map, footprint, corners, tiles_x, tiles_y, size):
    obs, width = footprint.shape
    nz = width - 2 * FP
    tiles = tiles_x * tiles_y
    vmem = pl.BlockSpec(memory_space=pltpu.VMEM)
    smem = pl.BlockSpec(memory_space=pltpu.SMEM)
    return pl.pallas_call(
        functools.partial(pack_kernel, tiles_x, tiles_y, size, nz),
        in_specs=[smem, smem, vmem, vmem],
        out_specs=vmem,
        out_shape=jax.ShapeDtypeStruct((tiles * CAP, LANES), jnp.float32),
        scratch_shapes=[pltpu.VMEM((LANES, obs), jnp.float32)],
        compiler_params=pltpu.CompilerParams(vmem_limit_bytes=VMEM_ALL),
        name="pack",
    )(number, owner_map, footprint.T, corners.T)


def prepare_kernel(
    tiles_x, tiles_y, size, nz, zb, number_ref, owner_ref, fp_ref, corner_ref,
    c_hbm, we_hbm, wn_hbm, k_hbm, sent_ref, e_ref, w_ref, n_ref, s_ref,
    m_ref, c_ref, we_ref, wn_ref, k_ref, sems,
):
    count, cols_x, cols_y = c_ref.shape[0], c_ref.shape[2], c_ref.shape[3]

    def fetch(i):
        at = pl.ds(i * zb, zb)
        return (
            pltpu.make_async_copy(c_hbm.at[:, at], c_ref.at[:, at], sems.at[0, i]),
            pltpu.make_async_copy(k_hbm.at[at], k_ref.at[at], sems.at[1, i]),
            pltpu.make_async_copy(wn_hbm.at[at], wn_ref.at[at], sems.at[2, i]),
            pltpu.make_async_copy(
                we_hbm.at[at, cols_x - 8 : cols_x], we_ref.at[at], sems.at[3, i]
            ),
        )

    for i in range(nz // zb):
        for copy in fetch(i):
            copy.start()

    pack_kernel(
        tiles_x, tiles_y, size, nz, number_ref, owner_ref, fp_ref, corner_ref, sent_ref, m_ref
    )

    def ends(slot, a_ref):
        e_ref[pl.ds(slot, 1), :] = a_ref[cols_x - 1 : cols_x, :]
        w_ref[pl.ds(slot, 1), :] = a_ref[0:1, :]
        flipped = a_ref[...].T
        n_ref[pl.ds(slot, 1), :] = flipped[cols_y - 1 : cols_y, :]
        s_ref[pl.ds(slot, 1), :] = flipped[0:1, :]

    def body(i, carry):
        for copy in fetch(i):
            copy.wait()
        for zi in range(zb):
            z = i * zb + zi
            for t in range(count):
                ends(t * nz + z, c_ref.at[t, z])
            ends(count * nz + z, k_ref.at[z])
            slot = (count + 1) * nz + z
            e_ref[pl.ds(slot, 1), :] = we_ref[z, 7:8, :]
            n_ref[pl.ds(slot, 1), :] = wn_ref[z].T[cols_y - 1 : cols_y, :]
        return carry

    lax.fori_loop(0, nz // zb, body, 0)


def prepare(
    number, owner_map, footprint, corners, tiles_x, tiles_y,
    tracers, wind_east, wind_north, diffusivity,
):
    count, nz, cols_x, cols_y = tracers.shape
    obs = footprint.shape[0]
    zb = 4
    f32 = jnp.float32
    flat = [(count + 2, cols_y), (count + 1, cols_y), (count + 2, cols_x), (count + 1, cols_x)]
    vmem = pl.BlockSpec(memory_space=pltpu.VMEM)
    smem = pl.BlockSpec(memory_space=pltpu.SMEM)
    return pl.pallas_call(
        functools.partial(prepare_kernel, tiles_x, tiles_y, (cols_x, cols_y), nz, zb),
        in_specs=[smem, smem, vmem, vmem, *[pl.BlockSpec(memory_space=pl.ANY)] * 4],
        out_specs=[vmem] * 5,
        out_shape=[
            jax.ShapeDtypeStruct((tiles_x * tiles_y * CAP, LANES), f32),
            *[jax.ShapeDtypeStruct((n * nz, width), f32) for n, width in flat],
        ],
        scratch_shapes=[
            pltpu.VMEM((LANES, obs), f32),
            pltpu.VMEM(tracers.shape, f32),
            pltpu.VMEM((nz, 8, cols_y), f32),
            pltpu.VMEM(wind_north.shape, f32),
            pltpu.VMEM(diffusivity.shape, f32),
            pltpu.SemaphoreType.DMA((4, nz // zb)),
        ],
        compiler_params=pltpu.CompilerParams(vmem_limit_bytes=VMEM_ALL),
        name="prepare",
    )(
        number, owner_map, footprint.T, corners.T, tracers, wind_east, wind_north, diffusivity
    )


def observe_kernel(nz, count, origin_ref, rows_ref, r_ref, out_ref, most_ref, near_ref, w_ref):
    cols = LANES
    chunk = w_ref.shape[1]
    scale = 1.0 / (FP * math.sqrt(nz))
    width = 2 * FP + nz
    lines = out_ref.shape[0]
    sources = rows_ref.shape[0] // CAP
    out_ref[...] = jnp.zeros_like(out_ref)
    heads = rows_ref[pl.ds(0, sources, stride=CAP), :]
    most = jnp.max(heads, axis=0, keepdims=True)
    most_ref[...] = jnp.broadcast_to(most, most_ref.shape).astype(jnp.int32)

    filled = 0
    for b in range(sources):
        near_ref[pl.ds(filled, CAP), :] = rows_ref[b * CAP : (b + 1) * CAP, :]
        filled += heads[b, width + 5].astype(jnp.int32)
    near_ref[pl.ds(filled, chunk), :] = jnp.zeros((chunk, LANES), jnp.float32)

    def body(step, carry):
        rows = near_ref[pl.ds(pl.multiple_of(step * chunk, chunk), chunk), :].T
        place = lax.broadcasted_iota(jnp.int32, (cols, chunk), 0)

        def along(profile, corner, origin):
            offset = place - (corner.astype(jnp.int32) - origin)
            inside = (offset >= 0) & (offset < FP)
            return jnp.where(inside, jnp.concatenate([profile] * (cols // FP), axis=0), 0.0)

        wy = along(rows[FP : 2 * FP], rows[width + 1 : width + 2], origin_ref[1])
        for z in range(nz):
            part = wy * rows[2 * FP + z : 2 * FP + z + 1]
            w_ref[z * cols : (z + 1) * cols, :] = part.astype(jnp.bfloat16)
        got = jnp.dot(r_ref[...], w_ref[...], preferred_element_type=jnp.float32)
        wx = along(rows[0:FP], rows[width : width + 1], origin_ref[0]) * scale
        values = [
            jnp.sum(got[t * cols : (t + 1) * cols] * wx, axis=0, keepdims=True)
            for t in range(count)
        ]
        values = jnp.concatenate(values * (8 // count), axis=0)
        owner = lax.broadcasted_iota(jnp.int32, (lines, chunk), 0) // count
        mine = owner == rows[width + 4 : width + 5].astype(jnp.int32)
        spread = jnp.where(mine, jnp.concatenate([values] * (lines // 8), axis=0), 0.0)
        high = spread.astype(jnp.bfloat16)
        low = (spread - high.astype(jnp.float32)).astype(jnp.bfloat16)
        obs = jnp.where(place == rows[width + 2 : width + 3].astype(jnp.int32), 1.0, 0.0)
        obs = obs.astype(jnp.bfloat16)
        across = (((1,), (1,)), ((), ()))
        out_ref[...] += lax.dot_general(
            high, obs, across, preferred_element_type=jnp.float32
        ) + lax.dot_general(low, obs, across, preferred_element_type=jnp.float32)
        return carry

    lax.fori_loop(0, (filled + chunk - 1) // chunk, body, 0)


def observe_scratch(rows, rounded_shape):
    return [
        pltpu.VMEM((rows + CHUNK, LANES), jnp.float32),
        pltpu.VMEM((rounded_shape[1], CHUNK), jnp.bfloat16),
    ]


def observed_shapes(sources, count):
    return [
        jax.ShapeDtypeStruct((sources * count, LANES), jnp.float32),
        jax.ShapeDtypeStruct((8, LANES), jnp.int32),
    ]


def observe(origin, rows, rounded, count, nz, sources):
    vmem = pl.BlockSpec(memory_space=pltpu.VMEM)
    smem = pl.BlockSpec(memory_space=pltpu.SMEM)
    return pl.pallas_call(
        functools.partial(observe_kernel, nz, count),
        in_specs=[smem, vmem, vmem],
        out_specs=[vmem, vmem],
        out_shape=observed_shapes(sources, count),
        scratch_shapes=observe_scratch(rows.shape[0], rounded.shape),
        compiler_params=pltpu.CompilerParams(vmem_limit_bytes=VMEM_MOST),
        name="observe",
    )(origin, rows, rounded)


PAD = 8


def step_kernel(
    nz, zb, place_ref, c_hbm, we_hbm, wn_hbm, k_hbm, em_ref, tag_ref,
    hw_ref, he_ref, hs_ref, hn_ref, rows_ref, out_hbm, r_hbm, parts_ref, most_ref,
    c_ref, we_ref, wn_ref, k_ref, ct_ref, wnt_ref, kt_ref, y_ref, out_ref, r_ref,
    near_ref, weight_ref, sems, out_sems, r_sem,
):
    count, _, cols_x, cols_y = c_hbm.shape
    slab = 32
    in_x, in_y = pl.ds(PAD, cols_x), pl.ds(PAD, cols_y)

    def fetch(i):
        at = pl.ds(i * zb, zb)
        return (
            pltpu.make_async_copy(c_hbm.at[:, at], c_ref.at[:, at, in_x], sems.at[0, i]),
            pltpu.make_async_copy(k_hbm.at[at], k_ref.at[at, in_x], sems.at[1, i]),
            pltpu.make_async_copy(we_hbm.at[at], we_ref.at[at, in_x], sems.at[2, i]),
            pltpu.make_async_copy(wn_hbm.at[at], wn_ref.at[at], sems.at[3, i]),
        )

    def send(i):
        at = pl.ds(i * zb, zb)
        return pltpu.make_async_copy(out_ref.at[:, at], out_hbm.at[:, at], out_sems.at[i])

    for i in range(nz // zb):
        for copy in fetch(i):
            copy.start()

    def surround(a_ref, low_ref, high_ref, slot):
        last = a_ref.shape[0] - PAD
        a_ref[PAD - 1 : PAD, :] = low_ref[pl.ds(slot, 1), :]
        if high_ref is not None:
            a_ref[last : last + 1, :] = high_ref[pl.ds(slot, 1), :]

    def three(a_ref, at):
        first = PAD + at
        return (
            a_ref[first : first + slab, :],
            a_ref[first + 1 : first + 1 + slab, :],
            a_ref[first - 1 : first - 1 + slab, :],
        )

    def coefficients(wind_ref, k_ref, at):
        wind, _, wind_m = three(wind_ref, at)
        k, k_p, k_m = three(k_ref, at)
        mix, mix_m = 0.5 * (k + k_p), 0.5 * (k + k_m)
        own = jnp.maximum(wind, 0.0) + mix - (jnp.minimum(wind_m, 0.0) - mix_m)
        return own, mix - jnp.minimum(wind, 0.0), jnp.maximum(wind_m, 0.0) + mix_m

    def body(i, carry):
        for copy in fetch(i):
            copy.wait()
        for zi in range(zb):
            z = i * zb + zi
            at_k, at_w = count * nz + z, (count + 1) * nz + z
            surround(k_ref.at[z], hw_ref, he_ref, at_k)
            surround(we_ref.at[z], hw_ref, None, at_w)
            kt_ref[zi, PAD : PAD + cols_y, :] = k_ref[z, PAD : PAD + cols_x, :].T
            surround(kt_ref.at[zi], hs_ref, hn_ref, at_k)
            wnt_ref[zi, PAD : PAD + cols_y, :] = wn_ref[z].T
            surround(wnt_ref.at[zi], hs_ref, None, at_w)
            for t in range(count):
                surround(c_ref.at[t, z], hw_ref, he_ref, t * nz + z)
                ct_ref[t, zi, PAD : PAD + cols_y, :] = c_ref[t, z, PAD : PAD + cols_x, :].T
                surround(ct_ref.at[t, zi], hs_ref, hn_ref, t * nz + z)
            for at in range(0, cols_y, slab):
                own, up, down = coefficients(wnt_ref.at[zi], kt_ref.at[zi], at)
                for t in range(count):
                    c, c_p, c_m = three(ct_ref.at[t, zi], at)
                    y_ref[t, zi, at : at + slab, :] = up * c_p + down * c_m - own * c
            for t in range(count):
                y_ref[t, zi] = y_ref[t, zi].T
            lanes = pl.ds(pl.multiple_of(z * cols_y, cols_y), cols_y)
            for at in range(0, cols_x, slab):
                own, up, down = coefficients(we_ref.at[z], k_ref.at[z], at)
                own = 1.0 - own
                rows = slice(at, at + slab)
                for t in range(count):
                    c, c_p, c_m = three(c_ref.at[t, z], at)
                    new = own * c + up * c_p + down * c_m + y_ref[t, zi, rows, :]
                    if zi == 0:
                        hit = (tag_ref[rows, :] == place_ref[2] + t) & (i == 0)
                        new = new + jnp.where(hit, em_ref[rows, :], 0.0)
                    out_ref[t, z, rows, :] = new
                    r_ref[t * cols_x + at : t * cols_x + at + slab, lanes] = new.astype(
                        jnp.bfloat16
                    )
        send(i).start()
        return carry

    lax.fori_loop(0, nz // zb, body, 0)
    keep = pltpu.make_async_copy(r_ref, r_hbm, r_sem)
    keep.start()
    observe_kernel(
        nz, count, place_ref, rows_ref, r_ref, parts_ref, most_ref, near_ref, weight_ref
    )
    for i in range(nz // zb):
        send(i).wait()
    keep.wait()


def advance(place, tracers, wind_east, wind_north, k, emission, tag, halos, rows, sources):
    count, nz, cols_x, cols_y = tracers.shape
    zb = 4
    f32 = jnp.float32
    vmem = pl.BlockSpec(memory_space=pltpu.VMEM)
    hbm = pl.BlockSpec(memory_space=pl.ANY)
    rounded = jax.ShapeDtypeStruct((count * cols_x, nz * cols_y), jnp.bfloat16)
    return pl.pallas_call(
        functools.partial(step_kernel, nz, zb),
        in_specs=[pl.BlockSpec(memory_space=pltpu.SMEM), *[hbm] * 4, *[vmem] * 7],
        out_specs=[hbm, hbm, vmem, vmem],
        out_shape=[
            jax.ShapeDtypeStruct(tracers.shape, f32),
            rounded,
            *observed_shapes(sources, count),
        ],
        scratch_shapes=[
            pltpu.VMEM((count, nz, cols_x + 2 * PAD, cols_y), f32),
            pltpu.VMEM((nz, cols_x + 2 * PAD, cols_y), f32),
            pltpu.VMEM((nz, cols_x, cols_y), f32),
            pltpu.VMEM((nz, cols_x + 2 * PAD, cols_y), f32),
            pltpu.VMEM((count, zb, cols_y + 2 * PAD, cols_x), f32),
            pltpu.VMEM((zb, cols_y + 2 * PAD, cols_x), f32),
            pltpu.VMEM((zb, cols_y + 2 * PAD, cols_x), f32),
            pltpu.VMEM((count, zb, cols_y, cols_x), f32),
            pltpu.VMEM(tracers.shape, f32),
            pltpu.VMEM(rounded.shape, rounded.dtype),
            *observe_scratch(rows.shape[0], rounded.shape),
            pltpu.SemaphoreType.DMA((4, nz // zb)),
            pltpu.SemaphoreType.DMA((nz // zb,)),
            pltpu.SemaphoreType.DMA,
        ],
        cost_estimate=pl.CostEstimate(
            flops=40 * tracers.size, bytes_accessed=13 << 20, transcendentals=0
        ),
        compiler_params=pltpu.CompilerParams(vmem_limit_bytes=VMEM_MOST),
        name="advance",
    )(place, tracers, wind_east, wind_north, k, emission, tag, *halos, rows)


def per_device(
    tracers, wind_east, wind_north, diffusivity, emission, region_tag, footprint, corners, owner_map
):
    count, nz, cols_x, cols_y = tracers.shape
    tiles_x, tiles_y = lax.axis_size("gx"), lax.axis_size("gy")
    tiles = tiles_x * tiles_y
    obs = footprint.shape[0]
    me = lax.axis_index(TILES)
    place = [lax.axis_index("gx") * cols_x, lax.axis_index("gy") * cols_y]
    place = jnp.stack([*place, lax.axis_index("tracer") * count]).astype(jnp.int32)

    def numbered(number):
        return jnp.stack([number, me]).astype(jnp.int32)

    sent, east, west, north, south = prepare(
        numbered(jnp.int32(0)), owner_map, footprint, corners, tiles_x, tiles_y,
        tracers, wind_east, wind_north, diffusivity,
    )

    def to_tiles(rows):
        rows = lax.all_to_all(rows.reshape(tiles, CAP, LANES), TILES, 0, 0)
        return rows.reshape(tiles * CAP, LANES)

    def to_owners(parts):
        return jnp.sum(lax.all_to_all(parts.reshape(tiles, count, obs), TILES, 0, 0), axis=0)

    rows = to_tiles(sent)
    up_x = [(i, i + 1) for i in range(tiles_x - 1)]
    up_y = [(i, i + 1) for i in range(tiles_y - 1)]
    halos = (
        lax.ppermute(east, "gx", up_x),
        lax.ppermute(west, "gx", [(b, a) for a, b in up_x]),
        lax.ppermute(north, "gy", up_y),
        lax.ppermute(south, "gy", [(b, a) for a, b in up_y]),
    )
    stepped, rounded, parts, most = advance(
        place, tracers, wind_east, wind_north, diffusivity, emission, region_tag, halos, rows, tiles
    )
    observed = to_owners(parts)

    def later_round(number, total):
        rows = to_tiles(
            pack(
                numbered(number), owner_map, footprint, corners, tiles_x, tiles_y, (cols_x, cols_y)
            )
        )
        parts, _ = observe(place, rows, rounded, count, nz, tiles)
        return total + to_owners(parts)

    rounds = (most[0, 2 * FP + nz + 3] + CAP - 1) // CAP
    observed = lax.fori_loop(jnp.int32(1), rounds, later_round, observed)
    return (stepped, observed)


def solution(mesh):
    return jax.shard_map(
        per_device,
        mesh=mesh,
        in_specs=(
            P("tracer", None, "gx", "gy"),
            P(None, "gx", "gy"),
            P(None, "gx", "gy"),
            P(None, "gx", "gy"),
            P("gx", "gy"),
            P("gx", "gy"),
            P(("gx", "gy"), None),
            P(("gx", "gy"), None),
            P(),
        ),
        out_specs=(P("tracer", None, "gx", "gy"), P("tracer", ("gx", "gy"))),
        check_vma=False,
    )
```

```python
import functools
import math

import jax
import jax.numpy as jnp
from jax import lax
from jax.experimental import pallas as pl
from jax.experimental.pallas import tpu as pltpu
from jax.sharding import PartitionSpec as P

FP = 32
CAP = 24
LANES = 128
CHUNK = 256
VMEM_ALL = 56 << 20
VMEM_MOST = 50 << 20
TILES = ("gx", "gy")


def pack_kernel(
    tiles_x, tiles_y, size, nz, number_ref, me_ref, owner_ref, fp_ref, corner_ref, out_ref, m_ref
):
    tiles = tiles_x * tiles_y
    obs = fp_ref.shape[1]
    width = 2 * FP + nz
    tile = lax.broadcasted_iota(jnp.int32, (tiles, obs), 0)
    first_x = (tile // tiles_y) * size[0]
    first_y = (tile % tiles_y) * size[1]
    x0 = corner_ref[0:1, :]
    y0 = corner_ref[1:2, :]
    touch = (
        (x0 < first_x + size[0])
        & (x0 + FP > first_x)
        & (y0 < first_y + size[1])
        & (y0 + FP > first_y)
    )
    ones = jnp.where(touch, 1.0, 0.0)
    earlier = lax.broadcasted_iota(jnp.int32, (obs, obs), 0) < lax.broadcasted_iota(
        jnp.int32, (obs, obs), 1
    )
    rank = jnp.dot(
        ones.astype(jnp.bfloat16),
        jnp.where(earlier, 1.0, 0.0).astype(jnp.bfloat16),
        preferred_element_type=jnp.float32,
    ).astype(jnp.int32)
    count = jnp.sum(ones, axis=1, keepdims=True)
    most = jnp.max(count, axis=0, keepdims=True)
    now = jnp.clip(count - (number_ref[0] * CAP).astype(jnp.float32), 0.0, CAP)
    slot = jnp.where(touch, rank - number_ref[0] * CAP, -1)
    which = lax.broadcasted_iota(jnp.int32, (tiles, CAP, obs), 1)
    pick = jnp.where(slot[:, None, :] == which, 1.0, 0.0).reshape(tiles * CAP, obs)
    pick = pick.astype(jnp.bfloat16)

    def rotated(profile, by):
        shift = 1
        while shift < FP:
            turn = (by & shift) != 0
            profile = jnp.where(turn, pltpu.roll(profile, shift, 0), profile)
            shift *= 2
        return profile

    m_ref[0:FP, :] = rotated(fp_ref[0:FP, :], x0)
    m_ref[FP : 2 * FP, :] = rotated(fp_ref[FP : 2 * FP, :], y0)
    m_ref[2 * FP : width, :] = fp_ref[2 * FP : width, :]
    m_ref[width:, :] = jnp.zeros_like(m_ref[width:, :])
    m_ref[width : width + 2, :] = corner_ref[...].astype(jnp.float32)
    m_ref[width + 2 : width + 3, :] = lax.broadcasted_iota(jnp.int32, (1, obs), 1).astype(
        jnp.float32
    )
    rows = m_ref[...].T
    lane = lax.broadcasted_iota(jnp.int32, rows.shape, 1)
    high = rows.astype(jnp.bfloat16)
    low = jnp.where(lane < 2 * FP, 0.0, rows - high.astype(jnp.float32)).astype(jnp.bfloat16)
    packed = jnp.dot(pick, high, preferred_element_type=jnp.float32) + jnp.dot(
        pick, low, preferred_element_type=jnp.float32
    )
    lane = lax.broadcasted_iota(jnp.int32, packed.shape, 1)
    packed = jnp.where(lane == width + 3, most, packed)
    owner = owner_ref[me_ref[0]].astype(jnp.float32)
    packed = jnp.where(lane == width + 4, owner, packed)
    now = jnp.broadcast_to(now[:, :, None], (tiles, CAP, LANES)).reshape(packed.shape)
    out_ref[...] = jnp.where(lane == width + 5, now, packed)


def pack(number, me, owner_map, footprint, corners, tiles_x, tiles_y, size):
    obs, width = footprint.shape
    nz = width - 2 * FP
    tiles = tiles_x * tiles_y
    vmem = pl.BlockSpec(memory_space=pltpu.VMEM)
    smem = pl.BlockSpec(memory_space=pltpu.SMEM)
    return pl.pallas_call(
        functools.partial(pack_kernel, tiles_x, tiles_y, size, nz),
        in_specs=[smem, smem, smem, vmem, vmem],
        out_specs=vmem,
        out_shape=jax.ShapeDtypeStruct((tiles * CAP, LANES), jnp.float32),
        scratch_shapes=[pltpu.VMEM((LANES, obs), jnp.float32)],
        compiler_params=pltpu.CompilerParams(vmem_limit_bytes=VMEM_ALL),
        name="pack",
    )(number, me, owner_map, footprint.T, corners.T)


def prepare_kernel(
    tiles_x, tiles_y, size, nz, zb, number_ref, me_ref, owner_ref, fp_ref, corner_ref,
    c_hbm, we_hbm, wn_hbm, k_hbm, sent_ref, xa_ref, xb_ref, ya_ref, yb_ref,
    m_ref, c_ref, we_ref, wn_ref, k_ref, sems,
):
    count, cols_x, cols_y = c_ref.shape[0], c_ref.shape[2], c_ref.shape[3]

    def fetch(i):
        at = pl.ds(i * zb, zb)
        return (
            pltpu.make_async_copy(c_hbm.at[:, at], c_ref.at[:, at], sems.at[0, i]),
            pltpu.make_async_copy(k_hbm.at[at], k_ref.at[at], sems.at[1, i]),
            pltpu.make_async_copy(wn_hbm.at[at], wn_ref.at[at], sems.at[2, i]),
            pltpu.make_async_copy(
                we_hbm.at[at, cols_x - 8 : cols_x], we_ref.at[at], sems.at[3, i]
            ),
        )

    for i in range(nz // zb):
        for copy in fetch(i):
            copy.start()

    pack_kernel(
        tiles_x, tiles_y, size, nz, number_ref, me_ref, owner_ref, fp_ref, corner_ref, sent_ref, m_ref
    )

    even_x = (me_ref[0] // tiles_y) % 2 == 0
    even_y = (me_ref[0] % tiles_y) % 2 == 0
    row_a = jnp.where(even_x, cols_x - 1, 0)
    row_b = cols_x - 1 - row_a

    def ends(slot, a_ref):
        xa_ref[pl.ds(slot, 1), :] = a_ref[pl.ds(row_a, 1), :]
        xb_ref[pl.ds(slot, 1), :] = a_ref[pl.ds(row_b, 1), :]
        flipped = a_ref[...].T
        low, high = flipped[0:1, :], flipped[cols_y - 1 : cols_y, :]
        ya_ref[pl.ds(slot, 1), :] = jnp.where(even_y, high, low)
        yb_ref[pl.ds(slot, 1), :] = jnp.where(even_y, low, high)

    def body(i, carry):
        for copy in fetch(i):
            copy.wait()
        for zi in range(zb):
            z = i * zb + zi
            for t in range(count):
                ends(t * nz + z, c_ref.at[t, z])
            ends(count * nz + z, k_ref.at[z])
            slot = (count + 1) * nz + z
            for to_ref in (xa_ref, xb_ref):
                to_ref[pl.ds(slot, 1), :] = we_ref[z, 7:8, :]
            last = wn_ref[z].T[cols_y - 1 : cols_y, :]
            for to_ref in (ya_ref, yb_ref):
                to_ref[pl.ds(slot, 1), :] = last
        return carry

    lax.fori_loop(0, nz // zb, body, 0)


def prepare(
    number, me, owner_map, footprint, corners, tiles_x, tiles_y,
    tracers, wind_east, wind_north, diffusivity,
):
    count, nz, cols_x, cols_y = tracers.shape
    obs = footprint.shape[0]
    zb = 4
    f32 = jnp.float32
    edge_rows = (count + 2) * nz
    vmem = pl.BlockSpec(memory_space=pltpu.VMEM)
    smem = pl.BlockSpec(memory_space=pltpu.SMEM)
    return pl.pallas_call(
        functools.partial(prepare_kernel, tiles_x, tiles_y, (cols_x, cols_y), nz, zb),
        in_specs=[smem, smem, smem, vmem, vmem, *[pl.BlockSpec(memory_space=pl.ANY)] * 4],
        out_specs=[vmem] * 5,
        out_shape=[
            jax.ShapeDtypeStruct((tiles_x * tiles_y * CAP, LANES), f32),
            *[jax.ShapeDtypeStruct((edge_rows, width), f32) for width in (cols_y, cols_y, cols_x, cols_x)],
        ],
        scratch_shapes=[
            pltpu.VMEM((LANES, obs), f32),
            pltpu.VMEM(tracers.shape, f32),
            pltpu.VMEM((nz, 8, cols_y), f32),
            pltpu.VMEM(wind_north.shape, f32),
            pltpu.VMEM(diffusivity.shape, f32),
            pltpu.SemaphoreType.DMA((4, nz // zb)),
        ],
        compiler_params=pltpu.CompilerParams(vmem_limit_bytes=VMEM_ALL),
        name="prepare",
    )(
        number, me, owner_map, footprint.T, corners.T, tracers, wind_east, wind_north, diffusivity
    )


def observe_kernel(nz, count, origin_ref, rows_ref, r_ref, out_ref, most_ref, near_ref, w_ref):
    cols = LANES
    chunk = w_ref.shape[1]
    scale = 1.0 / (FP * math.sqrt(nz))
    width = 2 * FP + nz
    lines = out_ref.shape[0]
    sources = rows_ref.shape[0] // CAP
    out_ref[...] = jnp.zeros_like(out_ref)
    heads = rows_ref[pl.ds(0, sources, stride=CAP), :]
    most = jnp.max(heads, axis=0, keepdims=True)
    most_ref[...] = jnp.broadcast_to(most, most_ref.shape).astype(jnp.int32)

    filled = 0
    for b in range(sources):
        near_ref[pl.ds(filled, CAP), :] = rows_ref[b * CAP : (b + 1) * CAP, :]
        filled += heads[b, width + 5].astype(jnp.int32)
    near_ref[pl.ds(filled, chunk), :] = jnp.zeros((chunk, LANES), jnp.float32)

    def body(step, carry):
        rows = near_ref[pl.ds(pl.multiple_of(step * chunk, chunk), chunk), :].T
        place = lax.broadcasted_iota(jnp.int32, (cols, chunk), 0)

        def along(profile, corner, origin):
            offset = place - (corner.astype(jnp.int32) - origin)
            inside = (offset >= 0) & (offset < FP)
            return jnp.where(inside, jnp.concatenate([profile] * (cols // FP), axis=0), 0.0)

        wy = along(rows[FP : 2 * FP], rows[width + 1 : width + 2], origin_ref[1])
        for z in range(nz):
            part = wy * rows[2 * FP + z : 2 * FP + z + 1]
            w_ref[z * cols : (z + 1) * cols, :] = part.astype(jnp.bfloat16)
        got = jnp.dot(r_ref[...], w_ref[...], preferred_element_type=jnp.float32)
        wx = along(rows[0:FP], rows[width : width + 1], origin_ref[0]) * scale
        values = [
            jnp.sum(got[t * cols : (t + 1) * cols] * wx, axis=0, keepdims=True)
            for t in range(count)
        ]
        values = jnp.concatenate(values * (8 // count), axis=0)
        owner = lax.broadcasted_iota(jnp.int32, (lines, chunk), 0) // count
        mine = owner == rows[width + 4 : width + 5].astype(jnp.int32)
        spread = jnp.where(mine, jnp.concatenate([values] * (lines // 8), axis=0), 0.0)
        high = spread.astype(jnp.bfloat16)
        low = (spread - high.astype(jnp.float32)).astype(jnp.bfloat16)
        obs = jnp.where(place == rows[width + 2 : width + 3].astype(jnp.int32), 1.0, 0.0)
        obs = obs.astype(jnp.bfloat16)
        across = (((1,), (1,)), ((), ()))
        out_ref[...] += lax.dot_general(
            high, obs, across, preferred_element_type=jnp.float32
        ) + lax.dot_general(low, obs, across, preferred_element_type=jnp.float32)
        return carry

    lax.fori_loop(0, (filled + chunk - 1) // chunk, body, 0)


def observe_scratch(rows, rounded_shape):
    return [
        pltpu.VMEM((rows + CHUNK, LANES), jnp.float32),
        pltpu.VMEM((rounded_shape[1], CHUNK), jnp.bfloat16),
    ]


def observed_shapes(sources, count):
    return [
        jax.ShapeDtypeStruct((sources * count, LANES), jnp.float32),
        jax.ShapeDtypeStruct((8, LANES), jnp.int32),
    ]


def observe(origin, rows, rounded, count, nz, sources):
    vmem = pl.BlockSpec(memory_space=pltpu.VMEM)
    smem = pl.BlockSpec(memory_space=pltpu.SMEM)
    return pl.pallas_call(
        functools.partial(observe_kernel, nz, count),
        in_specs=[smem, vmem, vmem],
        out_specs=[vmem, vmem],
        out_shape=observed_shapes(sources, count),
        scratch_shapes=observe_scratch(rows.shape[0], rounded.shape),
        compiler_params=pltpu.CompilerParams(vmem_limit_bytes=VMEM_MOST),
        name="observe",
    )(origin, rows, rounded)


PAD = 8


def step_kernel(
    nz, zb, place_ref, c_hbm, we_hbm, wn_hbm, k_hbm, em_ref, tag_ref,
    yb_ref, ya_ref, xb_ref, xa_ref, rows_ref, out_hbm, r_hbm, parts_ref, most_ref,
    c_ref, we_ref, wn_ref, k_ref, ct_ref, wnt_ref, kt_ref, y_ref, out_ref, r_ref,
    halo_x_ref, halo_y_ref, near_ref, weight_ref, sems, out_sems, r_sem,
):
    count, _, cols_x, cols_y = c_hbm.shape
    slab = 32
    in_x, in_y = pl.ds(PAD, cols_x), pl.ds(PAD, cols_y)

    def fetch(i):
        at = pl.ds(i * zb, zb)
        return (
            pltpu.make_async_copy(c_hbm.at[:, at], c_ref.at[:, at, in_x], sems.at[0, i]),
            pltpu.make_async_copy(k_hbm.at[at], k_ref.at[at, in_x], sems.at[1, i]),
            pltpu.make_async_copy(we_hbm.at[at], we_ref.at[at, in_x], sems.at[2, i]),
            pltpu.make_async_copy(wn_hbm.at[at], wn_ref.at[at], sems.at[3, i]),
        )

    def send(i):
        at = pl.ds(i * zb, zb)
        return pltpu.make_async_copy(out_ref.at[:, at], out_hbm.at[:, at], out_sems.at[i])

    for i in range(nz // zb):
        for copy in fetch(i):
            copy.start()

    side_x = 1 - (place_ref[0] // cols_x) % 2
    side_y = 1 - (place_ref[1] // cols_y) % 2
    halo_x_ref[side_x] = xa_ref[...]
    halo_x_ref[1 - side_x] = xb_ref[...]
    halo_y_ref[side_y] = ya_ref[...]
    halo_y_ref[1 - side_y] = yb_ref[...]
    hw_ref, he_ref = halo_x_ref.at[0], halo_x_ref.at[1]
    hs_ref, hn_ref = halo_y_ref.at[0], halo_y_ref.at[1]

    def surround(a_ref, low_ref, high_ref, slot):
        last = a_ref.shape[0] - PAD
        a_ref[PAD - 1 : PAD, :] = low_ref[pl.ds(slot, 1), :]
        if high_ref is not None:
            a_ref[last : last + 1, :] = high_ref[pl.ds(slot, 1), :]

    def three(a_ref, at):
        first = PAD + at
        return (
            a_ref[first : first + slab, :],
            a_ref[first + 1 : first + 1 + slab, :],
            a_ref[first - 1 : first - 1 + slab, :],
        )

    def coefficients(wind_ref, k_ref, at):
        wind, _, wind_m = three(wind_ref, at)
        k, k_p, k_m = three(k_ref, at)
        mix, mix_m = 0.5 * (k + k_p), 0.5 * (k + k_m)
        own = jnp.maximum(wind, 0.0) + mix - (jnp.minimum(wind_m, 0.0) - mix_m)
        return own, mix - jnp.minimum(wind, 0.0), jnp.maximum(wind_m, 0.0) + mix_m

    def body(i, carry):
        for copy in fetch(i):
            copy.wait()
        for zi in range(zb):
            z = i * zb + zi
            at_k, at_w = count * nz + z, (count + 1) * nz + z
            surround(k_ref.at[z], hw_ref, he_ref, at_k)
            surround(we_ref.at[z], hw_ref, None, at_w)
            kt_ref[zi, PAD : PAD + cols_y, :] = k_ref[z, PAD : PAD + cols_x, :].T
            surround(kt_ref.at[zi], hs_ref, hn_ref, at_k)
            wnt_ref[zi, PAD : PAD + cols_y, :] = wn_ref[z].T
            surround(wnt_ref.at[zi], hs_ref, None, at_w)
            for t in range(count):
                surround(c_ref.at[t, z], hw_ref, he_ref, t * nz + z)
                ct_ref[t, zi, PAD : PAD + cols_y, :] = c_ref[t, z, PAD : PAD + cols_x, :].T
                surround(ct_ref.at[t, zi], hs_ref, hn_ref, t * nz + z)
            for at in range(0, cols_y, slab):
                own, up, down = coefficients(wnt_ref.at[zi], kt_ref.at[zi], at)
                for t in range(count):
                    c, c_p, c_m = three(ct_ref.at[t, zi], at)
                    y_ref[t, zi, at : at + slab, :] = up * c_p + down * c_m - own * c
            for t in range(count):
                y_ref[t, zi] = y_ref[t, zi].T
            lanes = pl.ds(pl.multiple_of(z * cols_y, cols_y), cols_y)
            for at in range(0, cols_x, slab):
                own, up, down = coefficients(we_ref.at[z], k_ref.at[z], at)
                own = 1.0 - own
                rows = slice(at, at + slab)
                for t in range(count):
                    c, c_p, c_m = three(c_ref.at[t, z], at)
                    new = own * c + up * c_p + down * c_m + y_ref[t, zi, rows, :]
                    if zi == 0:
                        hit = (tag_ref[rows, :] == place_ref[2] + t) & (i == 0)
                        new = new + jnp.where(hit, em_ref[rows, :], 0.0)
                    out_ref[t, z, rows, :] = new
                    r_ref[t * cols_x + at : t * cols_x + at + slab, lanes] = new.astype(
                        jnp.bfloat16
                    )
        send(i).start()
        return carry

    lax.fori_loop(0, nz // zb, body, 0)
    keep = pltpu.make_async_copy(r_ref, r_hbm, r_sem)
    keep.start()
    observe_kernel(
        nz, count, place_ref, rows_ref, r_ref, parts_ref, most_ref, near_ref, weight_ref
    )
    for i in range(nz // zb):
        send(i).wait()
    keep.wait()


def advance(place, tracers, wind_east, wind_north, k, emission, tag, halos, rows, sources):
    count, nz, cols_x, cols_y = tracers.shape
    zb = 4
    f32 = jnp.float32
    vmem = pl.BlockSpec(memory_space=pltpu.VMEM)
    hbm = pl.BlockSpec(memory_space=pl.ANY)
    rounded = jax.ShapeDtypeStruct((count * cols_x, nz * cols_y), jnp.bfloat16)
    return pl.pallas_call(
        functools.partial(step_kernel, nz, zb),
        in_specs=[pl.BlockSpec(memory_space=pltpu.SMEM), *[hbm] * 4, *[vmem] * 7],
        out_specs=[hbm, hbm, vmem, vmem],
        out_shape=[
            jax.ShapeDtypeStruct(tracers.shape, f32),
            rounded,
            *observed_shapes(sources, count),
        ],
        scratch_shapes=[
            pltpu.VMEM((count, nz, cols_x + 2 * PAD, cols_y), f32),
            pltpu.VMEM((nz, cols_x + 2 * PAD, cols_y), f32),
            pltpu.VMEM((nz, cols_x, cols_y), f32),
            pltpu.VMEM((nz, cols_x + 2 * PAD, cols_y), f32),
            pltpu.VMEM((count, zb, cols_y + 2 * PAD, cols_x), f32),
            pltpu.VMEM((zb, cols_y + 2 * PAD, cols_x), f32),
            pltpu.VMEM((zb, cols_y + 2 * PAD, cols_x), f32),
            pltpu.VMEM((count, zb, cols_y, cols_x), f32),
            pltpu.VMEM(tracers.shape, f32),
            pltpu.VMEM(rounded.shape, rounded.dtype),
            pltpu.VMEM((2, *halos[0].shape), f32),
            pltpu.VMEM((2, *halos[2].shape), f32),
            *observe_scratch(rows.shape[0], rounded.shape),
            pltpu.SemaphoreType.DMA((4, nz // zb)),
            pltpu.SemaphoreType.DMA((nz // zb,)),
            pltpu.SemaphoreType.DMA,
        ],
        cost_estimate=pl.CostEstimate(
            flops=40 * tracers.size, bytes_accessed=13 << 20, transcendentals=0
        ),
        compiler_params=pltpu.CompilerParams(vmem_limit_bytes=VMEM_MOST),
        name="advance",
    )(place, tracers, wind_east, wind_north, k, emission, tag, *halos, rows)


def per_device(
    tracers, wind_east, wind_north, diffusivity, emission, region_tag, footprint, corners, owner_map
):
    count, nz, cols_x, cols_y = tracers.shape
    tiles_x, tiles_y = lax.axis_size("gx"), lax.axis_size("gy")
    tiles = tiles_x * tiles_y
    obs = footprint.shape[0]
    me = lax.axis_index(TILES).astype(jnp.int32).reshape(1)
    place = [lax.axis_index("gx") * cols_x, lax.axis_index("gy") * cols_y]
    place = jnp.stack([*place, lax.axis_index("tracer") * count]).astype(jnp.int32)

    sent, *edges = prepare(
        jnp.zeros((1,), jnp.int32), me, owner_map, footprint, corners, tiles_x, tiles_y,
        tracers, wind_east, wind_north, diffusivity,
    )

    def to_tiles(rows):
        rows = lax.all_to_all(rows.reshape(tiles, CAP, LANES), TILES, 0, 0)
        return rows.reshape(tiles * CAP, LANES)

    def to_owners(parts):
        return jnp.sum(lax.all_to_all(parts.reshape(tiles, count, obs), TILES, 0, 0), axis=0)

    rows = to_tiles(sent)
    def swap(edge, axis, first):
        pairs = [(i, i + 1) for i in range(first, lax.axis_size(axis) - 1, 2)]
        return lax.ppermute(edge, axis, pairs + [(b, a) for a, b in pairs])

    edge_xa, edge_xb, edge_ya, edge_yb = edges
    halos = (
        swap(edge_yb, "gy", 1), swap(edge_ya, "gy", 0), swap(edge_xb, "gx", 1), swap(edge_xa, "gx", 0)
    )
    stepped, rounded, parts, most = advance(
        place, tracers, wind_east, wind_north, diffusivity, emission, region_tag, halos, rows, tiles
    )
    observed = to_owners(parts)

    def later_round(number, total):
        rows = to_tiles(
            pack(
                number.reshape(1), me, owner_map, footprint, corners, tiles_x, tiles_y, (cols_x, cols_y)
            )
        )
        parts, _ = observe(place, rows, rounded, count, nz, tiles)
        return total + to_owners(parts)

    rounds = (most[0, 2 * FP + nz + 3] + CAP - 1) // CAP
    observed = lax.fori_loop(jnp.int32(1), rounds, later_round, observed)
    return (stepped, observed)


def solution(mesh):
    return jax.shard_map(
        per_device,
        mesh=mesh,
        in_specs=(
            P("tracer", None, "gx", "gy"),
            P(None, "gx", "gy"),
            P(None, "gx", "gy"),
            P(None, "gx", "gy"),
            P("gx", "gy"),
            P("gx", "gy"),
            P(("gx", "gy"), None),
            P(("gx", "gy"), None),
            P(),
        ),
        out_specs=(P("tracer", None, "gx", "gy"), P("tracer", ("gx", "gy"))),
        check_vma=False,
    )
```
